256 devices in a mesh: rep: 32 (over z_hi, x, core), fsdp: 8 (over y, z_lo).
Axes of the slice: x: 4, y: 4, z: 8 (z_hi: 4, z_lo: 2; z = z_hi * 2 + z_lo), core: 2. Of those that a mesh axis runs over, the one named last changes fastest.
Arguments:
- local_weights: bfloat16 [32, 5120, 512], P('rep', 'fsdp'), may hold values from -6 to 6
- global_weights: float32 [5120, 512], P('fsdp'), may hold values from -6 to 6
- momentum: float32 [5120, 512], P('fsdp'), may hold values from -6 to 6
- tokens: bfloat16 [131072, 5120], P(('rep', 'fsdp')), may hold values from -0.375 to 0.375
- key_grad: bfloat16 [131072, 512], P(('rep', 'fsdp')), may hold values from -6 to 6
Outputs:
- new_global: float32 [5120, 512], P('fsdp')
- new_momentum: float32 [5120, 512], P('fsdp')
- inner_keys: bfloat16 [131072, 512], P(('rep', 'fsdp'))
- weight_grad: bfloat16 [32, 5120, 512], P('rep', 'fsdp')
The draws below stay inside these ranges and needn't reach their ends.
All inputs are finite; a program needn't handle non-finite values.
Results may differ from the reference program's by a relative error of at most 0.0049.
Values may be sent and summed in bfloat16 or wider, within the bound.
No kernel may reach another device: no remote copies, remote signals or barrier semaphores. Data moves between devices by JAX's collectives and lax.ppermute only.
A program may use at most 128 MiB of HBM per device.

```python
import jax
import jax.numpy as jnp
from jax import lax

D = 5120
KW = 512
TOK_DEV = 512
REPLICAS = 32
TOKENS = 131072
N_REP = 32
N_FSDP = 8


def spiked(array, stream_key, source, target, parts, factor):
    owner, partner = [(jnp.arange(array.shape[axis_at]) // (array.shape[axis_at] // parts)).reshape([-1 if axis == axis_at else 1 for axis in range(array.ndim)]) for axis_at in (source, target)]
    chosen = jax.random.permutation(stream_key, parts)[partner]
    strong = (owner == chosen) | (owner == (partner + parts // 2) % parts)
    return jnp.where(strong, factor * array, array)


def shard_levels(key, dims, pieces, smallest, top_value):
    def one(axis_at, parts):
        heights = jax.random.uniform(jax.random.fold_in(jax.random.fold_in(key, 6), axis_at), (parts,), jnp.float32, smallest / len(pieces), top_value / len(pieces))
        return jnp.repeat(jnp.exp(heights), dims[axis_at] // parts).reshape((-1,) + (1,) * (len(dims) - axis_at - 1))

    factor_of = one(*pieces[0])
    for cut in pieces[1:]:
        factor_of = factor_of * one(*cut)
    return factor_of


def centred(stream_key, extent, width, most, split=(), kind=jnp.bfloat16):
    entries = jax.random.normal(stream_key, extent, jnp.float32) * width
    if len(split) > 0:
        entries = shard_levels(stream_key, extent, split, -0.22, 0.18) * entries
    return jnp.clip(entries, min=-most, max=most).astype(kind)


def gaussian_with(stream_key, extent, width, bound, cuts, heavy, dtype=jnp.bfloat16):
    result = width * jax.random.normal(stream_key, extent, jnp.float32)
    if cuts:
        result = result * shard_levels(stream_key, extent, cuts, -0.22, 0.18)
    return jnp.clip(spiked(result, jax.random.fold_in(stream_key, 3), *heavy), -bound, bound).astype(dtype)


def setup_inputs(seed: int = 0) -> dict:
    splits = jax.random.split(jax.random.key(seed), 6)
    return {
        "local_weights": centred(splits[0], (REPLICAS, D, KW), 1.0, 6.0, ((0, 32), (1, 8))),
        "global_weights": centred(splits[1], (D, KW), 1.0, 6.0, ((0, 8),), jnp.float32),
        "momentum": centred(splits[2], (D, KW), 1.0, 6.0, ((0, 8),), jnp.float32),
        "tokens": gaussian_with(splits[3], (TOKENS, D), (1.0 / D ** 0.5), 0.375, ((0, 256),), (0, 1, 256, 6.0)),
        "key_grad": centred(splits[4], (TOKENS, KW), 1.0, 6.0, ((0, 256),)),
    }


momentum_rate = 0.9
outer_rate = 0.7


def reference(local_weights, global_weights, momentum, tokens, key_grad):
    outer_grad = global_weights[None] - local_weights.astype(jnp.float32)
    average = jnp.sum(outer_grad, axis=0) / N_REP
    new_momentum = momentum_rate * momentum + average
    new_global = global_weights - outer_rate * (average + momentum_rate * new_momentum)
    start_weights = new_global.astype(jnp.bfloat16)
    group_rows = TOK_DEV * N_FSDP
    token_groups = tokens.reshape(N_REP, group_rows, D)
    grad_groups = key_grad.reshape(N_REP, group_rows, KW)

    def replica_step(inputs):
        inputs_tok, grad_one = inputs
        keys_one = jnp.dot(inputs_tok, start_weights, preferred_element_type=jnp.float32).astype(jnp.bfloat16)
        wgrad_one = lax.dot_general(inputs_tok, grad_one, (((0,), (0,)), ((), ())), preferred_element_type=jnp.float32).astype(jnp.bfloat16)
        return keys_one, wgrad_one

    inner_keys, weight_grad = lax.map(replica_step, (token_groups, grad_groups))
    return new_global, new_momentum, inner_keys.reshape(TOKENS, KW), weight_grad
```

```python
import jax
import jax.numpy as jnp
from jax import lax
from jax.experimental import pallas as pl
from jax.experimental.pallas import tpu as pltpu
from jax.sharding import PartitionSpec as P

momentum_rate = 0.9
outer_rate = 0.7

F32, BF16 = jnp.float32, jnp.bfloat16
AXES = ("rep", "fsdp")
SIZES = (4, 4, 2, 4, 2)
REPLICAS = 32
D, KW, SHARD = 5120, 512, 640
TOK = 512
ROWS, COLS = 160, 256
FIRST = 256
LATER = SHARD - FIRST


def shift(value, zh=0, x=0, core=0, y=0, zl=0):
    steps = (zh, x, core, y, zl)

    def index(place):
        n = 0
        for p, size in zip(place, SIZES):
            n = n * size + p
        return n

    pairs = []
    for a in range(4):
        for b in range(4):
            for c in range(2):
                for d in range(4):
                    for e in range(2):
                        place = (a, b, c, d, e)
                        to = tuple((p + s) % n for p, s, n in zip(place, steps, SIZES))
                        pairs.append((index(place), index(to)))
    return lax.ppermute(value, AXES, pairs)


def grad_kernel(order, tokens, key_grad, f0, f1, f2, f3, mine, other):
    step = pl.program_id(0)
    part = lax.dot_general(
        tokens[...], key_grad[...], (((0,), (0,)), ((), ())), preferred_element_type=F32
    ).astype(BF16)
    for k, ref in enumerate((f0, f1, f2, f3)):

        @pl.when(step // 2 == k)
        def _(ref=ref):
            ref[0] = part[:FIRST]

    @pl.when(step % 2 == 0)
    def _():
        mine[0] = part[FIRST:]

    @pl.when(step % 2 == 1)
    def _():
        other[0] = part[FIRST:]


def grad_parts(order, tokens, key_grad):
    def first(k):
        return pl.BlockSpec((1, FIRST, KW), lambda s, o: (jnp.clip(s - 2 * k, 0, 1), 0, 0))

    later = pl.BlockSpec((1, LATER, KW), lambda s, o: (s // 2, 0, 0))
    return pl.pallas_call(
        grad_kernel,
        grid_spec=pltpu.PrefetchScalarGridSpec(
            num_scalar_prefetch=1,
            grid=(8,),
            in_specs=[
                pl.BlockSpec((TOK, SHARD), lambda s, o: (0, o[s])),
                pl.BlockSpec((TOK, KW), lambda s, o: (0, 0)),
            ],
            out_specs=[first(0), first(1), first(2), first(3), later, later],
        ),
        out_shape=[jax.ShapeDtypeStruct((2, FIRST, KW), BF16)] * 4
        + [jax.ShapeDtypeStruct((4, LATER, KW), BF16)] * 2,
        compiler_params=pltpu.CompilerParams(vmem_limit_bytes=32 << 20),
        cost_estimate=pl.CostEstimate(flops=2 * TOK * D * KW, bytes_accessed=11 << 20, transcendentals=0),
    )(order, tokens, key_grad)


def pair_kernel(order, g, l0, l1, own, p1, p2, p3):
    step = pl.program_id(0)
    total = 2.0 * g[...] - l0[...].astype(F32) - l1[...].astype(F32)

    @pl.when(step == 0)
    def _():
        own[...] = total

    for k, ref in enumerate((p1, p2, p3)):

        @pl.when(step == k + 1)
        def _(ref=ref):
            ref[...] = total.astype(BF16)


def pair_sums(order, g, l0, l1):
    block = pl.BlockSpec((ROWS, COLS), lambda s, o: (o[16 + s], o[24]))
    out = pl.BlockSpec((ROWS, COLS), lambda s, o: (0, 0))
    return pl.pallas_call(
        pair_kernel,
        grid_spec=pltpu.PrefetchScalarGridSpec(
            num_scalar_prefetch=1, grid=(4,), in_specs=[block] * 3, out_specs=[out] * 4
        ),
        out_shape=[jax.ShapeDtypeStruct((ROWS, COLS), F32)]
        + [jax.ShapeDtypeStruct((ROWS, COLS), BF16)] * 3,
    )(order, g, l0, l1)


def step_kernel(order, own, r1, r2, r3, g, m, average, start):
    avg = (own[...] + r1[...].astype(F32) + r2[...].astype(F32) + r3[...].astype(F32)) / REPLICAS
    new_m = momentum_rate * m[...] + avg
    new_g = g[...] - outer_rate * (avg + momentum_rate * new_m)
    average[...] = avg
    start[...] = new_g.astype(BF16)


def outer_step(order, own, r1, r2, r3, g, m):
    here = pl.BlockSpec((ROWS, COLS), lambda s, o: (0, 0))
    block = pl.BlockSpec((ROWS, COLS), lambda s, o: (o[16], o[24]))
    return pl.pallas_call(
        step_kernel,
        grid_spec=pltpu.PrefetchScalarGridSpec(
            num_scalar_prefetch=1, grid=(1,), in_specs=[here] * 4 + [block] * 2, out_specs=[here] * 2
        ),
        out_shape=[
            jax.ShapeDtypeStruct((ROWS, COLS), F32),
            jax.ShapeDtypeStruct((ROWS, COLS), BF16),
        ],
    )(order, own, r1, r2, r3, g, m)


def update_kernel(order, average, g, m, new_global, new_momentum):
    avg = average[0]
    new_m = momentum_rate * m[...] + avg
    new_momentum[...] = new_m
    new_global[...] = g[...] - outer_rate * (avg + momentum_rate * new_m)


def update(order, average, g, m):
    block = pl.BlockSpec(
        (ROWS, COLS), lambda h, s, o: (o[20 + s], (o[24] + h) % 2)
    )
    return pl.pallas_call(
        update_kernel,
        grid_spec=pltpu.PrefetchScalarGridSpec(
            num_scalar_prefetch=1,
            grid=(2, 4),
            in_specs=[
                pl.BlockSpec((1, ROWS, COLS), lambda h, s, o: (h * 4 + s, 0, 0)),
                block,
                block,
            ],
            out_specs=[block] * 2,
        ),
        out_shape=[jax.ShapeDtypeStruct((SHARD, KW), F32)] * 2,
    )(order, average, g, m)


def keys_kernel(order, tokens, tokens_other, w0, w1, w2, w3, keys, keys_other, weights, total, total_other):
    step = pl.program_id(0)
    for k, ref in enumerate((w0, w1, w2, w3)):
        weights[pl.ds(pl.multiple_of(order[20 + k] * ROWS, ROWS), ROWS), :] = ref[0]

    @pl.when(step == 0)
    def _():
        total[...] = jnp.zeros_like(total)
        total_other[...] = jnp.zeros_like(total_other)

    total[...] += jnp.dot(tokens[...], weights[...], preferred_element_type=F32)
    total_other[...] += jnp.dot(tokens_other[...], weights[...], preferred_element_type=F32)

    @pl.when(step == 7)
    def _():
        keys[...] = total[...].astype(BF16)
        keys_other[...] = total_other[...].astype(BF16)


def keys_of(order, tokens, tokens_other, blocks):
    rows = pl.BlockSpec((TOK, SHARD), lambda s, o: (0, o[8 + s]))
    block = pl.BlockSpec((1, ROWS, COLS), lambda s, o: (s, 0, 0))
    out = pl.BlockSpec((TOK, COLS), lambda s, o: (0, 0))
    return pl.pallas_call(
        keys_kernel,
        grid_spec=pltpu.PrefetchScalarGridSpec(
            num_scalar_prefetch=1,
            grid=(8,),
            in_specs=[rows] * 2 + [block] * 4,
            out_specs=[out] * 2,
            scratch_shapes=[
                pltpu.VMEM((SHARD, COLS), BF16),
                pltpu.VMEM((TOK, COLS), F32),
                pltpu.VMEM((TOK, COLS), F32),
            ],
        ),
        out_shape=[jax.ShapeDtypeStruct((TOK, COLS), BF16)] * 2,
        compiler_params=pltpu.CompilerParams(vmem_limit_bytes=32 << 20),
        cost_estimate=pl.CostEstimate(flops=2 * TOK * D * KW, bytes_accessed=14 << 20, transcendentals=0),
    )(order, tokens, tokens_other, *blocks)


def per_device(local_weights, global_weights, momentum, tokens, key_grad):
    g, m, local = global_weights, momentum, local_weights[0]
    rep, fsdp = lax.axis_index("rep"), lax.axis_index("fsdp")
    core, x, y, zl = rep % 2, rep // 2 % 4, fsdp // 2, fsdp % 2
    four, two = jnp.arange(4), jnp.arange(2)
    order = jnp.concatenate(
        [
            (((y + four) % 4)[:, None] * 2 + (zl + two)[None] % 2).reshape(8),
            (((y - four) % 4)[:, None] * 2 + (zl + two)[None] % 2).reshape(8),
            (x + four) % 4,
            (x - four) % 4,
            core[None],
        ]
    ).astype(jnp.int32)

    local_other = shift(local, core=1)
    tokens_other = shift(tokens, core=1)

    f0, f1, f2, f3, mine, other = grad_parts(order, tokens, key_grad)

    own, p1, p2, p3 = pair_sums(order, g, local, local_other)
    r1, r2, r3 = (shift(p, x=k + 1) for k, p in enumerate((p1, p2, p3)))

    f1, f2, f3 = (shift(f, y=k + 1) for k, f in enumerate((f1, f2, f3)))
    got = shift(other, zl=1)

    chips = own + r1.astype(F32) + r2.astype(F32) + r3.astype(F32)
    sent = chips.astype(BF16)
    q1, q2, q3 = (shift(sent, zh=k) for k in (1, 2, 3))
    average, start = outer_step(order, chips, q1, q2, q3, g, m)

    pair = jnp.stack([start, shift(start, zl=1)])
    shards = jnp.concatenate([pair] + [shift(pair, y=k) for k in (1, 2, 3)])
    blocks = [shards] + [shift(shards, x=k) for k in (1, 2, 3)]

    half = jnp.stack([average] + [shift(average, x=k) for k in (1, 2, 3)])
    whole = jnp.concatenate([half, shift(half, core=1)])
    new_global, new_momentum = update(order, whole, g, m)

    f_sum = f0.astype(F32) + f1.astype(F32) + f2.astype(F32) + f3.astype(F32)
    f_got = shift(f_sum[1].astype(BF16), zl=1)
    l_sum = mine.astype(F32) + got.astype(F32)
    l_got = [shift(l_sum[k].astype(BF16), y=k) for k in (1, 2, 3)]
    weight_grad = jnp.concatenate(
        [
            f_sum[0] + f_got.astype(F32),
            l_sum[0] + l_got[0].astype(F32) + l_got[1].astype(F32) + l_got[2].astype(F32),
        ]
    ).astype(BF16)[None]

    keys, keys_other = keys_of(order, tokens, tokens_other, blocks)
    keys_got = shift(keys_other, core=1)
    inner_keys = jnp.where(
        core == 0,
        jnp.concatenate([keys, keys_got], axis=1),
        jnp.concatenate([keys_got, keys], axis=1),
    )
    return (new_global, new_momentum, inner_keys, weight_grad)


def solution(mesh):
    placed = (
        P("rep", "fsdp", None),
        P("fsdp", None),
        P("fsdp", None),
        P(("rep", "fsdp"), None),
        P(("rep", "fsdp"), None),
    )
    return jax.shard_map(
        per_device,
        mesh=mesh,
        in_specs=placed,
        out_specs=(
            P("fsdp", None),
            P("fsdp", None),
            P(("rep", "fsdp"), None),
            P("rep", "fsdp", None),
        ),
        check_vma=False,
    )
```

```python
import jax
import jax.numpy as jnp
from jax import lax
from jax.experimental import pallas as pl
from jax.experimental.pallas import tpu as pltpu
from jax.sharding import PartitionSpec as P

momentum_rate = 0.9
outer_rate = 0.7

F32, BF16 = jnp.float32, jnp.bfloat16
AXES = ("rep", "fsdp")
SIZES = (4, 4, 2, 4, 2)
REPLICAS = 32
D, KW, SHARD = 5120, 512, 640
TOK = 512
ROWS, COLS = 160, 256
HALF = SHARD // 2


def shift(value, zh=0, x=0, core=0, y=0, zl=0):
    steps = (zh, x, core, y, zl)

    def index(place):
        n = 0
        for p, size in zip(place, SIZES):
            n = n * size + p
        return n

    pairs = []
    for a in range(4):
        for b in range(4):
            for c in range(2):
                for d in range(4):
                    for e in range(2):
                        place = (a, b, c, d, e)
                        to = tuple((p + s) % n for p, s, n in zip(place, steps, SIZES))
                        pairs.append((index(place), index(to)))
    return lax.ppermute(value, AXES, pairs)


def after(value, *others):
    return lax.optimization_barrier((value, *others))[0]


def share(tokens, key_grad):
    return lax.dot_general(
        tokens[...], key_grad[...], (((0,), (0,)), ((), ())), preferred_element_type=F32
    ).astype(BF16)


def far_kernel(order, tokens, key_grad, low, high):
    part = share(tokens, key_grad)
    for z in range(2):
        low[z] = part[z * SHARD : z * SHARD + HALF]
        high[z] = part[z * SHARD + HALF : (z + 1) * SHARD]


def far_part(order, tokens, key_grad):
    return pl.pallas_call(
        far_kernel,
        grid_spec=pltpu.PrefetchScalarGridSpec(
            num_scalar_prefetch=1,
            grid=(1,),
            in_specs=[
                pl.BlockSpec((TOK, 2 * SHARD), lambda s, o: (0, o[2])),
                pl.BlockSpec((TOK, KW), lambda s, o: (0, 0)),
            ],
            out_specs=[pl.BlockSpec((2, HALF, KW), lambda s, o: (0, 0, 0))] * 2,
        ),
        out_shape=[jax.ShapeDtypeStruct((2, HALF, KW), BF16)] * 2,
        compiler_params=pltpu.CompilerParams(vmem_limit_bytes=32 << 20),
        cost_estimate=pl.CostEstimate(flops=TOK * D * KW // 2, bytes_accessed=3 << 20, transcendentals=0),
    )(order, tokens, key_grad)


def near_kernel(order, tokens, key_grad, up, down, here):
    step = pl.program_id(0)
    part = share(tokens, key_grad).reshape(2, SHARD, KW)
    for k, ref in enumerate((up, down, here)):

        @pl.when(step == k)
        def _(ref=ref):
            ref[...] = part


def near_parts(order, tokens, key_grad):
    out = pl.BlockSpec((2, SHARD, KW), lambda s, o: (0, 0, 0))
    return pl.pallas_call(
        near_kernel,
        grid_spec=pltpu.PrefetchScalarGridSpec(
            num_scalar_prefetch=1,
            grid=(3,),
            in_specs=[
                pl.BlockSpec((TOK, 2 * SHARD), lambda s, o: (0, o[8 + s])),
                pl.BlockSpec((TOK, KW), lambda s, o: (0, 0)),
            ],
            out_specs=[out] * 3,
        ),
        out_shape=[jax.ShapeDtypeStruct((2, SHARD, KW), BF16)] * 3,
        compiler_params=pltpu.CompilerParams(vmem_limit_bytes=48 << 20),
        cost_estimate=pl.CostEstimate(flops=3 * TOK * D * KW // 2, bytes_accessed=8 << 20, transcendentals=0),
    )(order, tokens, key_grad)


def pair_kernel(order, g, l0, l1, own, p1, p2, p3):
    for k, ref in enumerate((own, p1, p2, p3)):
        rows = pl.ds(pl.multiple_of(order[16 + k] * ROWS, ROWS), ROWS)
        total = 2.0 * g[rows, :] - l0[rows, :].astype(F32) - l1[rows, :].astype(F32)
        ref[...] = total.astype(ref.dtype)


def pair_sums(order, g, l0, l1):
    block = pl.BlockSpec((SHARD, COLS), lambda s, o: (0, o[24]))
    out = pl.BlockSpec((ROWS, COLS), lambda s, o: (0, 0))
    return pl.pallas_call(
        pair_kernel,
        grid_spec=pltpu.PrefetchScalarGridSpec(
            num_scalar_prefetch=1, grid=(1,), in_specs=[block] * 3, out_specs=[out] * 4
        ),
        out_shape=[jax.ShapeDtypeStruct((ROWS, COLS), F32)]
        + [jax.ShapeDtypeStruct((ROWS, COLS), BF16)] * 3,
    )(order, g, l0, l1)


def step_kernel(order, own, r1, r2, r3, g, m, average, start):
    avg = (own[...] + r1[...].astype(F32) + r2[...].astype(F32) + r3[...].astype(F32)) / REPLICAS
    new_m = momentum_rate * m[...] + avg
    new_g = g[...] - outer_rate * (avg + momentum_rate * new_m)
    average[...] = avg
    start[...] = new_g.astype(BF16)


def outer_step(order, own, r1, r2, r3, g, m):
    here = pl.BlockSpec((ROWS, COLS), lambda s, o: (0, 0))
    block = pl.BlockSpec((ROWS, COLS), lambda s, o: (o[16], o[24]))
    return pl.pallas_call(
        step_kernel,
        grid_spec=pltpu.PrefetchScalarGridSpec(
            num_scalar_prefetch=1, grid=(1,), in_specs=[here] * 4 + [block] * 2, out_specs=[here] * 2
        ),
        out_shape=[
            jax.ShapeDtypeStruct((ROWS, COLS), F32),
            jax.ShapeDtypeStruct((ROWS, COLS), BF16),
        ],
    )(order, own, r1, r2, r3, g, m)


def join_kernel(*refs):
    *parts, out = refs
    at = 0
    for ref in parts:
        n = ref.shape[0]
        out[at : at + n] = ref[...]
        at += n


def join(*parts):
    n = sum(p.shape[0] for p in parts)
    return pl.pallas_call(
        join_kernel,
        out_shape=jax.ShapeDtypeStruct((n, *parts[0].shape[1:]), parts[0].dtype),
    )(*parts)


def update_kernel(average, g, m, new_global, new_momentum):
    for h in range(2):
        cols = slice(h * COLS, (h + 1) * COLS)
        new_m = momentum_rate * m[:, cols] + average[h]
        new_momentum[:, cols] = new_m
        new_global[:, cols] = g[:, cols] - outer_rate * (average[h] + momentum_rate * new_m)


def update(average, g, m):
    block = pl.BlockSpec((ROWS, KW), lambda s: (s, 0))
    return pl.pallas_call(
        update_kernel,
        grid=(4,),
        in_specs=[pl.BlockSpec((2, ROWS, COLS), lambda s: (s, 0, 0)), block, block],
        out_specs=[block] * 2,
        out_shape=[jax.ShapeDtypeStruct((SHARD, KW), F32)] * 2,
    )(average, g, m)


def keys_kernel(order, tokens, w0, w1, w2, w3, keys, weights):
    @pl.when(pl.program_id(0) == 0)
    def _():
        for d in range(4):
            for z in range(2):
                for k, ref in enumerate((w0, w1, w2, w3)):
                    at = order[4 + d] * (2 * SHARD) + order[12 + z] * SHARD + order[20 + k] * ROWS
                    weights[pl.ds(pl.multiple_of(at, ROWS), ROWS), :] = ref[2 * d + z]

    keys[0] = jnp.dot(tokens[0], weights[...], preferred_element_type=F32).astype(BF16)


def keys_of(order, tokens, blocks):
    part = 4
    rows = pl.BlockSpec((1, TOK // part, D), lambda s, o: (s // part, s % part, 0))
    whole = pl.BlockSpec((8, ROWS, COLS), lambda s, o: (0, 0, 0))
    return pl.pallas_call(
        keys_kernel,
        grid_spec=pltpu.PrefetchScalarGridSpec(
            num_scalar_prefetch=1,
            grid=(2 * part,),
            in_specs=[rows] + [whole] * 4,
            out_specs=pl.BlockSpec((1, TOK // part, COLS), lambda s, o: (s // part, s % part, 0)),
            scratch_shapes=[pltpu.VMEM((D, COLS), BF16)],
        ),
        out_shape=jax.ShapeDtypeStruct((2, TOK, COLS), BF16),
        compiler_params=pltpu.CompilerParams(vmem_limit_bytes=32 << 20),
        cost_estimate=pl.CostEstimate(flops=2 * TOK * D * KW, bytes_accessed=14 << 20, transcendentals=0),
    )(order, tokens, *blocks)


def per_device(local_weights, global_weights, momentum, tokens, key_grad):
    g, m, local = global_weights, momentum, local_weights[0]
    rep, fsdp = lax.axis_index("rep"), lax.axis_index("fsdp")
    core, x, y, zl = rep % 2, rep // 2 % 4, fsdp // 2, fsdp % 2
    four = jnp.arange(4)
    order = jnp.concatenate(
        [
            (y + four) % 4,
            (y - four) % 4,
            (y + jnp.array([1, 3, 0, 0])) % 4,
            (zl + four) % 2,
            (x + four) % 4,
            (x - four) % 4,
            core[None],
        ]
    ).astype(jnp.int32)

    local_other = shift(local, core=1)
    pairs = lax.all_gather(tokens, "rep", axis_index_groups=[[2 * k, 2 * k + 1] for k in range(16)])

    low, high = far_part(order, tokens, key_grad)
    low, high = shift(low, y=1), shift(high, y=-1)

    own, p1, p2, p3 = pair_sums(order, g, local, local_other)
    r1, r2, r3 = (shift(p, x=k + 1) for k, p in enumerate((p1, p2, p3)))

    up, down, here = near_parts(order, after(tokens, p1), key_grad)

    chips = own + r1.astype(F32) + r2.astype(F32) + r3.astype(F32)
    sent = chips.astype(BF16)
    q1, q2, q3 = (shift(sent, zh=k) for k in (1, 2, 3))

    low, high = after(low, sent), after(high, sent)
    up = jnp.concatenate([up[:, :HALF] + low, up[:, HALF:]], axis=1)
    down = jnp.concatenate([down[:, :HALF], down[:, HALF:] + high], axis=1)
    up, down = shift(up, y=1), shift(down, y=-1)

    average, start = outer_step(order, chips, q1, q2, q3, g, m)

    pair = join(start[None], shift(start, zl=1)[None])
    shards = join(pair, *(shift(pair, y=k) for k in (1, 2, 3)))
    blocks = [shards] + [shift(shards, x=k) for k in (1, 2, 3)]

    whole = lax.all_gather(
        average, "rep", axis_index_groups=[[8 * k + j for j in range(8)] for k in range(4)]
    )
    new_global, new_momentum = update(whole, g, m)

    rows = here.astype(F32) + up.astype(F32) + down.astype(F32)
    got = shift(lax.dynamic_index_in_dim(rows, 1 - zl, 0, False).astype(BF16), zl=1)
    weight_grad = (lax.dynamic_index_in_dim(rows, zl, 0, False) + got.astype(F32)).astype(BF16)[None]

    keys = keys_of(order, pairs, blocks)
    keys_got = shift(lax.dynamic_index_in_dim(keys, 1 - core, 0, False), core=1)
    keys = lax.dynamic_index_in_dim(keys, core, 0, False)
    inner_keys = jnp.where(
        core == 0,
        jnp.concatenate([keys, keys_got], axis=1),
        jnp.concatenate([keys_got, keys], axis=1),
    )
    return (new_global, new_momentum, inner_keys, weight_grad)


def solution(mesh):
    placed = (
        P("rep", "fsdp", None),
        P("fsdp", None),
        P("fsdp", None),
        P(("rep", "fsdp"), None),
        P(("rep", "fsdp"), None),
    )
    return jax.shard_map(
        per_device,
        mesh=mesh,
        in_specs=placed,
        out_specs=(
            P("fsdp", None),
            P("fsdp", None),
            P(("rep", "fsdp"), None),
            P("rep", "fsdp", None),
        ),
        check_vma=False,
    )
```

```python
import functools

import jax
import jax.numpy as jnp
from jax import lax
from jax.experimental import pallas as pl
from jax.experimental.pallas import tpu as pltpu
from jax.sharding import PartitionSpec as P

momentum_rate = 0.9
outer_rate = 0.7

F32, BF16 = jnp.float32, jnp.bfloat16
AXES = ("rep", "fsdp")
SIZES = (4, 4, 2, 4, 2)
REPLICAS = 32
D, KW, SHARD = 5120, 512, 640
TOK = 512
ROWS, COLS = 160, 256


def shift(value, zh=0, x=0, core=0, y=0, zl=0, both_ways=False):
    steps = (zh, x, core, y, zl)

    def index(place):
        n = 0
        for p, size in zip(place, SIZES):
            n = n * size + p
        return n

    pairs = []
    for a in range(4):
        for b in range(4):
            for c in range(2):
                for d in range(4):
                    for e in range(2):
                        place = (a, b, c, d, e)
                        sign = -1 if both_ways and c == 1 else 1
                        to = tuple((p + sign * s) % n for p, s, n in zip(place, steps, SIZES))
                        pairs.append((index(place), index(to)))
    return lax.ppermute(value, AXES, pairs)


def after(value, *others):
    return lax.optimization_barrier((value, *others))[0]


def grant(mib):
    return pltpu.CompilerParams(vmem_limit_bytes=mib << 20)


def grad_kernel(at, sizes, order, tokens, key_grad, *refs):
    outs, held, sem = refs[: len(sizes)], refs[-2], refs[-1]
    copies = []
    for k, i in enumerate(at):
        columns = pl.ds(pl.multiple_of(order[i] * SHARD, SHARD), SHARD)
        copies.append(pltpu.make_async_copy(tokens.at[:, columns], held.at[k], sem.at[k]))
        copies[-1].start()
    places = [(out, j) for out, n in zip(outs, sizes) for j in range(n)]
    for k, (out, j) in enumerate(places):
        copies[k].wait()
        out[j] = lax.dot_general(
            held[k], key_grad[...], (((0,), (0,)), ((), ())), preferred_element_type=F32
        ).astype(BF16)


def grad_parts(order, at, sizes, tokens, key_grad):
    n = len(at)
    here = pl.BlockSpec(memory_space=pltpu.VMEM)
    return pl.pallas_call(
        functools.partial(grad_kernel, at, sizes),
        in_specs=[
            pl.BlockSpec(memory_space=pltpu.SMEM),
            pl.BlockSpec(memory_space=pltpu.HBM),
            here,
        ],
        out_specs=[here] * len(sizes),
        out_shape=[jax.ShapeDtypeStruct((k, SHARD, KW), BF16) for k in sizes],
        scratch_shapes=[pltpu.VMEM((n, TOK, SHARD), BF16), pltpu.SemaphoreType.DMA((n,))],
        compiler_params=grant(4 + 3 * n),
        cost_estimate=pl.CostEstimate(
            flops=2 * n * TOK * SHARD * KW, bytes_accessed=n * 1310720, transcendentals=0
        ),
    )(order, tokens, key_grad)


def pair_kernel(order, g, l0, l1, own, p1, p2, p3):
    for k, ref in enumerate((own, p1, p2, p3)):
        rows = pl.ds(pl.multiple_of(order[16 + k] * ROWS, ROWS), ROWS)
        total = 2.0 * g[rows, :] - l0[rows, :].astype(F32) - l1[rows, :].astype(F32)
        ref[...] = total.astype(ref.dtype)


def pair_sums(order, g, l0, l1):
    block = pl.BlockSpec((SHARD, COLS), lambda s, o: (0, o[24]))
    out = pl.BlockSpec((ROWS, COLS), lambda s, o: (0, 0))
    return pl.pallas_call(
        pair_kernel,
        grid_spec=pltpu.PrefetchScalarGridSpec(
            num_scalar_prefetch=1, grid=(1,), in_specs=[block] * 3, out_specs=[out] * 4
        ),
        out_shape=[jax.ShapeDtypeStruct((ROWS, COLS), F32)]
        + [jax.ShapeDtypeStruct((ROWS, COLS), BF16)] * 3,
        compiler_params=grant(6),
    )(order, g, l0, l1)


def step_kernel(order, own, r1, r2, r3, g, m, average, start):
    avg = (own[...] + r1[...].astype(F32) + r2[...].astype(F32) + r3[...].astype(F32)) / REPLICAS
    new_m = momentum_rate * m[...] + avg
    new_g = g[...] - outer_rate * (avg + momentum_rate * new_m)
    average[...] = avg
    start[...] = new_g.astype(BF16)


def outer_step(order, own, r1, r2, r3, g, m):
    here = pl.BlockSpec((ROWS, COLS), lambda s, o: (0, 0))
    block = pl.BlockSpec((ROWS, COLS), lambda s, o: (o[16], o[24]))
    return pl.pallas_call(
        step_kernel,
        grid_spec=pltpu.PrefetchScalarGridSpec(
            num_scalar_prefetch=1, grid=(1,), in_specs=[here] * 4 + [block] * 2, out_specs=[here] * 2
        ),
        out_shape=[
            jax.ShapeDtypeStruct((ROWS, COLS), F32),
            jax.ShapeDtypeStruct((ROWS, COLS), BF16),
        ],
        compiler_params=grant(4),
    )(order, own, r1, r2, r3, g, m)


def join_kernel(*refs):
    *parts, out = refs
    at = 0
    for ref in parts:
        n = ref.shape[0]
        out[at : at + n] = ref[...]
        at += n


def join(*parts):
    n = sum(p.shape[0] for p in parts)
    return pl.pallas_call(
        join_kernel,
        out_shape=jax.ShapeDtypeStruct((n, *parts[0].shape[1:]), parts[0].dtype),
        compiler_params=grant(4),
    )(*parts)


def update_kernel(order, average, g, m, new_global, new_momentum):
    for h in range(2):
        cols = slice(h * COLS, (h + 1) * COLS)
        new_m = momentum_rate * m[:, cols] + average[h]
        new_momentum[:, cols] = new_m
        new_global[:, cols] = g[:, cols] - outer_rate * (average[h] + momentum_rate * new_m)


def update(order, average, g, m):
    block = pl.BlockSpec((ROWS, KW), lambda s, o: (o[28 + s], 0))
    return pl.pallas_call(
        update_kernel,
        grid_spec=pltpu.PrefetchScalarGridSpec(
            num_scalar_prefetch=1,
            grid=(4,),
            in_specs=[pl.BlockSpec((2, ROWS, COLS), lambda s, o: (s, 0, 0)), block, block],
            out_specs=[block] * 2,
        ),
        out_shape=[jax.ShapeDtypeStruct((SHARD, KW), F32)] * 2,
        compiler_params=grant(8),
    )(order, average, g, m)


def keys_kernel(order, tokens, w0, w1, w2, w3, keys, weights, held, sem):
    places = [(h, slice(k * COLS, (k + 1) * COLS)) for h in range(2) for k in range(2)]
    copies = []
    for n, (h, rows) in enumerate(places):
        copies.append(pltpu.make_async_copy(tokens.at[h, rows], held.at[n], sem.at[n]))
        copies[-1].start()
    for d in range(4):
        for z in range(2):
            for k, ref in enumerate((w0, w1, w2, w3)):
                at = order[4 + d] * (2 * SHARD) + order[12 + z] * SHARD + order[20 + k] * ROWS
                weights[pl.ds(pl.multiple_of(at, ROWS), ROWS), :] = ref[2 * d + z]
    for n, (h, rows) in enumerate(places):
        copies[n].wait()
        keys[h, rows] = jnp.dot(held[n], weights[...], preferred_element_type=F32).astype(BF16)


def keys_of(order, tokens, blocks):
    here = pl.BlockSpec(memory_space=pltpu.VMEM)
    return pl.pallas_call(
        keys_kernel,
        in_specs=[pl.BlockSpec(memory_space=pltpu.SMEM), pl.BlockSpec(memory_space=pltpu.HBM)]
        + [here] * 4,
        out_specs=here,
        scratch_shapes=[
            pltpu.VMEM((D, COLS), BF16),
            pltpu.VMEM((4, COLS, D), BF16),
            pltpu.SemaphoreType.DMA((4,)),
        ],
        out_shape=jax.ShapeDtypeStruct((2, TOK, COLS), BF16),
        compiler_params=grant(24),
        cost_estimate=pl.CostEstimate(flops=2 * TOK * D * KW, bytes_accessed=14 << 20, transcendentals=0),
    )(order, tokens, *blocks)


def per_device(local_weights, global_weights, momentum, tokens, key_grad):
    g, m, local = global_weights, momentum, local_weights[0]
    rep, fsdp = lax.axis_index("rep"), lax.axis_index("fsdp")
    core, x, y, zl = rep % 2, rep // 2 % 4, fsdp // 2, fsdp % 2
    odd = rep // 8 % 2
    four = jnp.arange(4)
    way = 1 - 2 * core
    piece = x + 2 * odd

    def shards_of(y):
        return (y % 4) * 2 + (zl + jnp.arange(2)) % 2

    order = jnp.concatenate(
        [
            shards_of(y + 2),
            shards_of(y - way),
            (y - four) % 4,
            shards_of(y + way),
            shards_of(y),
            (zl + four) % 2,
            (piece + four) % 4,
            (piece - four) % 4,
            core + 0 * four,
            (four + 2 * odd) % 4,
        ]
    ).astype(jnp.int32)

    local_other = shift(local, core=1)
    pairs = lax.all_gather(tokens, "rep", axis_index_groups=[[2 * k, 2 * k + 1] for k in range(16)])

    (far,) = grad_parts(order, (0, 1), (2,), tokens, key_grad)
    far_got = shift(far, y=1, both_ways=True)

    local_other = after(local_other, far)
    own, p1, p2, p3 = pair_sums(order, g, local, local_other)
    r1, r2, r3 = (shift(p, x=k + 1) for k, p in enumerate((p1, p2, p3)))

    (direct,) = grad_parts(order, (2, 3), (2,), after(tokens, p1), key_grad)
    direct_got = shift(direct, y=-1, both_ways=True)

    chips = own + after(r1, direct).astype(F32) + r2.astype(F32) + r3.astype(F32)
    sent = chips.astype(BF16)
    q1, q2, q3 = (shift(sent, zh=k, x=2 * (k % 2)) for k in (1, 2, 3))

    on_own, on_other, here = grad_parts(
        order, (8, 9, 10, 11), (1, 1, 2), after(tokens, sent), key_grad
    )
    on_other = on_other[0] + far_got[1]
    on_other_got = shift(on_other, y=1, both_ways=True)

    average, start = outer_step(order, chips, after(q1, on_other, here), q2, q3, g, m)
    whole = lax.all_gather(
        average, "rep", axis_index_groups=[[8 * k + j for j in range(8)] for k in range(4)]
    )

    pair = join(start[None], shift(start, zl=1)[None])
    on_own = on_own[0] + after(far_got, pair)[0]
    on_own_got = shift(on_own, y=1, both_ways=True)
    shards = join(pair, *(shift(pair, y=k) for k in (1, 2, 3)))
    shards, pairs = lax.optimization_barrier((shards, pairs))
    blocks = [
        shards,
        shift(shards, x=1),
        shift(shards, zh=1, both_ways=True),
        shift(shards, x=-1),
    ]

    grad_sent = here[1].astype(F32) + direct_got[1].astype(F32) + on_other_got.astype(F32)
    grad_got = shift(grad_sent.astype(BF16), zl=1)

    new_global, new_momentum = update(order, after(whole, shards), g, m)

    grad_kept = here[0].astype(F32) + direct_got[0].astype(F32) + on_own_got.astype(F32)
    weight_grad = (grad_kept + grad_got.astype(F32)).astype(BF16)[None]

    *blocks, new_global, weight_grad = lax.optimization_barrier((*blocks, new_global, weight_grad))
    keys = keys_of(order, pairs, blocks)
    keys_got = shift(lax.dynamic_index_in_dim(keys, 1 - core, 0, False), core=1)
    keys = lax.dynamic_index_in_dim(keys, core, 0, False)
    inner_keys = jnp.where(
        core == 0,
        jnp.concatenate([keys, keys_got], axis=1),
        jnp.concatenate([keys_got, keys], axis=1),
    )
    return (new_global, new_momentum, inner_keys, weight_grad)


def solution(mesh):
    placed = (
        P("rep", "fsdp", None),
        P("fsdp", None),
        P("fsdp", None),
        P(("rep", "fsdp"), None),
        P(("rep", "fsdp"), None),
    )
    return jax.shard_map(
        per_device,
        mesh=mesh,
        in_specs=placed,
        out_specs=(
            P("fsdp", None),
            P("fsdp", None),
            P(("rep", "fsdp"), None),
            P("rep", "fsdp", None),
        ),
        check_vma=False,
    )
```

```python
import functools
import itertools

import jax
import jax.numpy as jnp
from jax import lax
from jax.experimental import pallas as pl
from jax.experimental.pallas import tpu as pltpu
from jax.sharding import PartitionSpec as P

momentum_rate = 0.9
outer_rate = 0.7

F32, BF16 = jnp.float32, jnp.bfloat16
AXES = ("rep", "fsdp")
SIZES = (4, 4, 2, 4, 2)
REPLICAS = 32
D, KW, SHARD = 5120, 512, 640
TOK = 512
ROWS, COLS = 160, 256


def send(value, target):
    pairs = []
    for place in itertools.product(*map(range, SIZES)):
        index = [0, 0]
        for k, where in enumerate((place, target(*place))):
            for p, size in zip(where, SIZES):
                index[k] = index[k] * size + p % size
        pairs.append(tuple(index))
    return lax.ppermute(value, AXES, pairs)


def shift(value, zh=0, x=0, core=0, y=0, zl=0, both_ways=False):
    def target(a, b, c, d, e):
        sign = -1 if both_ways and c == 1 else 1
        return a + sign * zh, b + sign * x, c + core, d + sign * y, e + zl

    return send(value, target)


def across(value):
    return send(value, lambda a, b, c, d, e: (a - 1 if e == 0 else a + 1, b, c, d, 1 - e))


def after(value, *others):
    return lax.optimization_barrier((value, *others))[0]


def grant(mib):
    return pltpu.CompilerParams(vmem_limit_bytes=mib << 20)


def grad_kernel(at, sizes, order, tokens, key_grad, *refs):
    outs, held, sem = refs[: len(sizes)], refs[-2], refs[-1]
    copies = []
    for k, i in enumerate(at):
        columns = pl.ds(pl.multiple_of(order[i] * SHARD, SHARD), SHARD)
        copies.append(pltpu.make_async_copy(tokens.at[:, columns], held.at[k], sem.at[k]))
        copies[-1].start()
    places = [(out, j) for out, n in zip(outs, sizes) for j in range(n)]
    for k, (out, j) in enumerate(places):
        copies[k].wait()
        out[j] = lax.dot_general(
            held[k], key_grad[...], (((0,), (0,)), ((), ())), preferred_element_type=F32
        ).astype(BF16)


def grad_parts(order, at, sizes, tokens, key_grad):
    n = len(at)
    here = pl.BlockSpec(memory_space=pltpu.VMEM)
    return pl.pallas_call(
        functools.partial(grad_kernel, at, sizes),
        in_specs=[
            pl.BlockSpec(memory_space=pltpu.SMEM),
            pl.BlockSpec(memory_space=pltpu.HBM),
            here,
        ],
        out_specs=[here] * len(sizes),
        out_shape=[jax.ShapeDtypeStruct((k, SHARD, KW), BF16) for k in sizes],
        scratch_shapes=[pltpu.VMEM((n, TOK, SHARD), BF16), pltpu.SemaphoreType.DMA((n,))],
        compiler_params=grant(4 + 3 * n),
        cost_estimate=pl.CostEstimate(
            flops=2 * n * TOK * SHARD * KW, bytes_accessed=n * 1310720, transcendentals=0
        ),
    )(order, tokens, key_grad)


def base_kernel(order, g, l, base):
    base[...] = 2.0 * g[...] - l[...].astype(F32)


def base_of(order, g, l):
    block = pl.BlockSpec((SHARD, COLS), lambda s, o: (0, o[24]))
    return pl.pallas_call(
        base_kernel,
        grid_spec=pltpu.PrefetchScalarGridSpec(
            num_scalar_prefetch=1,
            grid=(1,),
            in_specs=[block] * 2,
            out_specs=pl.BlockSpec((SHARD, COLS), lambda s, o: (0, 0)),
        ),
        out_shape=jax.ShapeDtypeStruct((SHARD, COLS), F32),
        compiler_params=grant(6),
    )(order, g, l)


def pair_kernel(order, base, l1, own, p1, p2, p3):
    for k, ref in enumerate((own, p1, p2, p3)):
        rows = pl.ds(pl.multiple_of(order[16 + k] * ROWS, ROWS), ROWS)
        ref[...] = (base[rows, :] - l1[rows, :].astype(F32)).astype(ref.dtype)


def pair_sums(order, base, l1):
    whole = pl.BlockSpec((SHARD, COLS), lambda s, o: (0, 0))
    block = pl.BlockSpec((SHARD, COLS), lambda s, o: (0, o[24]))
    out = pl.BlockSpec((ROWS, COLS), lambda s, o: (0, 0))
    return pl.pallas_call(
        pair_kernel,
        grid_spec=pltpu.PrefetchScalarGridSpec(
            num_scalar_prefetch=1, grid=(1,), in_specs=[whole, block], out_specs=[out] * 4
        ),
        out_shape=[jax.ShapeDtypeStruct((ROWS, COLS), F32)]
        + [jax.ShapeDtypeStruct((ROWS, COLS), BF16)] * 3,
        compiler_params=grant(6),
    )(order, base, l1)


def step_kernel(order, own, r1, r2, r3, g, m, average, start):
    avg = (own[...] + r1[...].astype(F32) + r2[...].astype(F32) + r3[...].astype(F32)) / REPLICAS
    new_m = momentum_rate * m[...] + avg
    new_g = g[...] - outer_rate * (avg + momentum_rate * new_m)
    average[...] = avg
    start[...] = new_g.astype(BF16)


def outer_step(order, own, r1, r2, r3, g, m):
    here = pl.BlockSpec((ROWS, COLS), lambda s, o: (0, 0))
    block = pl.BlockSpec((ROWS, COLS), lambda s, o: (o[16], o[24]))
    return pl.pallas_call(
        step_kernel,
        grid_spec=pltpu.PrefetchScalarGridSpec(
            num_scalar_prefetch=1, grid=(1,), in_specs=[here] * 4 + [block] * 2, out_specs=[here] * 2
        ),
        out_shape=[
            jax.ShapeDtypeStruct((ROWS, COLS), F32),
            jax.ShapeDtypeStruct((ROWS, COLS), BF16),
        ],
        compiler_params=grant(4),
    )(order, own, r1, r2, r3, g, m)


def join_kernel(*refs):
    *parts, out = refs
    at = 0
    for ref in parts:
        n = ref.shape[0]
        out[at : at + n] = ref[...]
        at += n


def join(*parts):
    n = sum(p.shape[0] for p in parts)
    return pl.pallas_call(
        join_kernel,
        out_shape=jax.ShapeDtypeStruct((n, *parts[0].shape[1:]), parts[0].dtype),
        compiler_params=grant(4),
    )(*parts)


def update_kernel(order, average, average_other, g, m, new_global, new_momentum):
    mine = order[24] == 0
    for h in range(2):
        cols = slice(h * COLS, (h + 1) * COLS)
        avg = jnp.where(mine == (h == 0), average[0], average_other[0])
        new_m = momentum_rate * m[:, cols] + avg
        new_momentum[:, cols] = new_m
        new_global[:, cols] = g[:, cols] - outer_rate * (avg + momentum_rate * new_m)


def update(order, average, average_other, g, m):
    block = pl.BlockSpec((ROWS, KW), lambda s, o: (o[28 + s], 0))
    part = pl.BlockSpec((1, ROWS, COLS), lambda s, o: (s, 0, 0))
    return pl.pallas_call(
        update_kernel,
        grid_spec=pltpu.PrefetchScalarGridSpec(
            num_scalar_prefetch=1,
            grid=(4,),
            in_specs=[part, part, block, block],
            out_specs=[block] * 2,
        ),
        out_shape=[jax.ShapeDtypeStruct((SHARD, KW), F32)] * 2,
        compiler_params=grant(8),
    )(order, average, average_other, g, m)


def hold_kernel(a, b, a_held, b_held, sem):
    copies = []
    for k, (src, dst) in enumerate(((a, a_held), (b, b_held))):
        for h in range(2):
            rows = pl.ds(h * COLS, COLS)
            copies.append(pltpu.make_async_copy(src.at[rows], dst.at[rows], sem.at[2 * k + h]))
            copies[-1].start()
    for copy in copies:
        copy.wait()


def hold(a, b):
    return pl.pallas_call(
        hold_kernel,
        in_specs=[pl.BlockSpec(memory_space=pl.ANY)] * 2,
        out_specs=[pl.BlockSpec(memory_space=pltpu.VMEM)] * 2,
        out_shape=[pltpu.VMEM((TOK, D), BF16)] * 2,
        scratch_shapes=[pltpu.SemaphoreType.DMA((4,))],
        compiler_params=grant(1),
    )(a, b)


def keys_kernel(order, tokens, tokens_other, w0, w1, w2, w3, keys, keys_other, weights):
    for d in range(4):
        for z in range(2):
            for k, ref in enumerate((w0, w1, w2, w3)):
                zl = order[12 + (z + (k == 2)) % 2]
                at = order[4 + d] * (2 * SHARD) + zl * SHARD + order[20 + k] * ROWS
                weights[pl.ds(pl.multiple_of(at, ROWS), ROWS), :] = ref[2 * d + z]
    for src, out in ((tokens_other, keys_other), (tokens, keys)):
        out[...] = jnp.dot(src[...], weights[...], preferred_element_type=F32).astype(BF16)


def keys_of(order, tokens, tokens_other, blocks):
    here = pl.BlockSpec(memory_space=pltpu.VMEM)
    return pl.pallas_call(
        keys_kernel,
        in_specs=[pl.BlockSpec(memory_space=pltpu.SMEM)] + [here] * 6,
        out_specs=[here] * 2,
        scratch_shapes=[pltpu.VMEM((D, COLS), BF16)],
        out_shape=[jax.ShapeDtypeStruct((TOK, COLS), BF16)] * 2,
        compiler_params=grant(24),
        cost_estimate=pl.CostEstimate(flops=20 * TOK * D * KW, bytes_accessed=14 << 20, transcendentals=0),
    )(order, tokens, tokens_other, *blocks)


def per_device(local_weights, global_weights, momentum, tokens, key_grad):
    g, m, local = global_weights, momentum, local_weights[0]
    rep, fsdp = lax.axis_index("rep"), lax.axis_index("fsdp")
    core, x, y, zl = rep % 2, rep // 2 % 4, fsdp // 2, fsdp % 2
    four = jnp.arange(4)
    way = 1 - 2 * core
    piece = x ^ (2 * zl)

    def shards_of(y):
        return (y % 4) * 2 + (zl + jnp.arange(2)) % 2

    order = jnp.concatenate(
        [
            shards_of(y + 2),
            shards_of(y - way),
            (y - four) % 4,
            shards_of(y + way),
            shards_of(y),
            (zl + four) % 2,
            (piece + four) % 4,
            (piece - four) % 4,
            core + 0 * four,
            piece ^ four,
        ]
    ).astype(jnp.int32)

    local_other = shift(local, core=1)
    base = base_of(order, g, local)
    local_other = after(local_other, base)
    tokens_other = shift(after(tokens, local_other), core=1)

    own, p1, p2, p3 = pair_sums(order, base, local_other)
    r1, r2, r3 = (shift(p, x=k + 1) for k, p in enumerate((p1, p2, p3)))

    (direct,) = grad_parts(order, (2, 3), (2,), after(tokens, p1), key_grad)
    direct_got = shift(direct, y=-1, both_ways=True)

    chips = own + after(r1, direct).astype(F32) + r2.astype(F32) + r3.astype(F32)
    sent = chips.astype(BF16)
    q1, q2, q3 = (shift(sent, zh=k) for k in (1, 2, 3))

    (far,) = grad_parts(order, (0, 1), (2,), after(tokens, sent), key_grad)
    far_got = shift(far, y=1, both_ways=True)
    on_own, on_other, here = grad_parts(
        order, (8, 9, 10, 11), (1, 1, 2), after(tokens, far), key_grad
    )

    q1, tokens_other = lax.optimization_barrier((after(q1, here), tokens_other))
    average, start = outer_step(order, chips, q1, q2, q3, g, m)

    start_other = shift(start, zl=1, x=2)
    average_1 = send(after(average, start), lambda a, b, c, d, e: (a, b ^ 1, c, d, e))
    pair = join(start[None], after(start_other, average_1)[None])
    average_1 = join(average[None], average_1[None])
    average_2 = send(after(average_1, pair), lambda a, b, c, d, e: (a, b ^ 2, c, d, e))
    shards = join(after(pair, average_2), *(shift(pair, y=k) for k in (1, 2, 3)))
    blocks = [shards, shift(shards, x=1), across(shards), shift(shards, x=-1)]

    on_other = on_other[0] + after(far_got, shards)[1]
    on_other_got = shift(on_other, y=1, both_ways=True)
    on_own = on_own[0] + far_got[0]
    on_own_got = shift(after(on_own, on_other), y=1, both_ways=True)

    average_2 = join(average_1, average_2)
    new_global, new_momentum = update(order, average_2, shift(average_2, core=1), g, m)

    grad_sent = here[1].astype(F32) + direct_got[1].astype(F32) + on_other_got.astype(F32)
    grad_got = shift(grad_sent.astype(BF16), zl=1)

    tokens, tokens_other = hold(after(tokens, shards), tokens_other)

    grad_kept = here[0].astype(F32) + direct_got[0].astype(F32) + on_own_got.astype(F32)
    weight_grad = (grad_kept + grad_got.astype(F32)).astype(BF16)[None]

    *blocks, new_global, tokens = lax.optimization_barrier((*blocks, new_global, tokens))
    keys, keys_other = keys_of(order, tokens, tokens_other, blocks)
    keys_got = shift(keys_other, core=1)
    inner_keys = jnp.where(
        core == 0,
        jnp.concatenate([keys, keys_got], axis=1),
        jnp.concatenate([keys_got, keys], axis=1),
    )
    return (new_global, new_momentum, inner_keys, weight_grad)


def solution(mesh):
    placed = (
        P("rep", "fsdp", None),
        P("fsdp", None),
        P("fsdp", None),
        P(("rep", "fsdp"), None),
        P(("rep", "fsdp"), None),
    )
    return jax.shard_map(
        per_device,
        mesh=mesh,
        in_specs=placed,
        out_specs=(
            P("fsdp", None),
            P("fsdp", None),
            P(("rep", "fsdp"), None),
            P("rep", "fsdp", None),
        ),
        check_vma=False,
    )
```

```python
import functools
import itertools

import jax
import jax.numpy as jnp
from jax import lax
from jax.experimental import pallas as pl
from jax.experimental.pallas import tpu as pltpu
from jax.sharding import PartitionSpec as P

momentum_rate = 0.9
outer_rate = 0.7

F32, BF16 = jnp.float32, jnp.bfloat16
AXES = ("rep", "fsdp")
SIZES = (4, 4, 2, 4, 2)
REPLICAS = 32
D, KW, SHARD = 5120, 512, 640
TOK = 512
ROWS, COLS = 160, 256


def send(value, target):
    pairs = []
    for place in itertools.product(*map(range, SIZES)):
        index = [0, 0]
        for k, where in enumerate((place, target(*place))):
            for p, size in zip(where, SIZES):
                index[k] = index[k] * size + p % size
        pairs.append(tuple(index))
    return lax.ppermute(value, AXES, pairs)


def shift(value, zh=0, x=0, core=0, y=0, zl=0, both_ways=False):
    def target(a, b, c, d, e):
        sign = -1 if both_ways and c == 1 else 1
        return a + sign * zh, b + sign * x, c + core, d + sign * y, e + zl

    return send(value, target)


def flip(value, zh=0, x=0):
    return send(value, lambda a, b, c, d, e: (a ^ zh, b ^ x, c, d, e))


def across(value):
    return send(value, lambda a, b, c, d, e: (a - 1 if e == 0 else a + 1, b, c, d, 1 - e))


def after(value, *others):
    return lax.optimization_barrier((value, *others))[0]


def grant(mib):
    return pltpu.CompilerParams(vmem_limit_bytes=mib << 20)


def in_hbm(value):
    return pltpu.with_memory_space_constraint(value, pltpu.HBM)


def grad_kernel(at, sizes, order, tokens, key_grad, *refs):
    outs, held, held_grad, sem = refs[: len(sizes)], *refs[len(sizes) :]
    copies = [pltpu.make_async_copy(key_grad, held_grad, sem.at[len(at)])]
    for k, i in enumerate(at):
        columns = pl.ds(pl.multiple_of(order[i] * SHARD, SHARD), SHARD)
        copies.append(pltpu.make_async_copy(tokens.at[:, columns], held.at[k], sem.at[k]))
    for copy in copies:
        copy.start()
    copies[0].wait()
    places = [(out, j) for out, n in zip(outs, sizes) for j in range(n)]
    for k, (out, j) in enumerate(places):
        copies[k + 1].wait()
        out[j] = lax.dot_general(
            held[k], held_grad[...], (((0,), (0,)), ((), ())), preferred_element_type=F32
        ).astype(BF16)


def grad_parts(order, at, sizes, tokens, key_grad):
    n = len(at)
    here = pl.BlockSpec(memory_space=pltpu.VMEM)
    hbm = pl.BlockSpec(memory_space=pltpu.HBM)
    return pl.pallas_call(
        functools.partial(grad_kernel, at, sizes),
        in_specs=[pl.BlockSpec(memory_space=pltpu.SMEM), hbm, hbm],
        out_specs=[here] * len(sizes),
        out_shape=[jax.ShapeDtypeStruct((k, SHARD, KW), BF16) for k in sizes],
        scratch_shapes=[
            pltpu.VMEM((n, TOK, SHARD), BF16),
            pltpu.VMEM((TOK, KW), BF16),
            pltpu.SemaphoreType.DMA((n + 1,)),
        ],
        compiler_params=grant(5 + 3 * n),
        cost_estimate=pl.CostEstimate(
            flops=2 * n * TOK * SHARD * KW, bytes_accessed=n * 1310720, transcendentals=0
        ),
    )(order, in_hbm(tokens), in_hbm(key_grad))


def base_kernel(order, g, l, base):
    base[...] = 2.0 * g[...] - l[...].astype(F32)


def base_of(order, g, l):
    block = pl.BlockSpec((SHARD, COLS), lambda s, o: (0, o[24]))
    return pl.pallas_call(
        base_kernel,
        grid_spec=pltpu.PrefetchScalarGridSpec(
            num_scalar_prefetch=1,
            grid=(1,),
            in_specs=[block] * 2,
            out_specs=pl.BlockSpec((SHARD, COLS), lambda s, o: (0, 0)),
        ),
        out_shape=jax.ShapeDtypeStruct((SHARD, COLS), F32),
        compiler_params=grant(6),
    )(order, in_hbm(g), in_hbm(l))


def pair_kernel(order, base, l1, own, p1, p2, p3):
    for k, ref in enumerate((own, p1, p2, p3)):
        rows = pl.ds(pl.multiple_of(order[16 + k] * ROWS, ROWS), ROWS)
        ref[...] = (base[rows, :] - l1[rows, :].astype(F32)).astype(ref.dtype)


def pair_sums(order, base, l1):
    whole = pl.BlockSpec((SHARD, COLS), lambda s, o: (0, 0))
    block = pl.BlockSpec((SHARD, COLS), lambda s, o: (0, o[24]))
    out = pl.BlockSpec((ROWS, COLS), lambda s, o: (0, 0))
    return pl.pallas_call(
        pair_kernel,
        grid_spec=pltpu.PrefetchScalarGridSpec(
            num_scalar_prefetch=1, grid=(1,), in_specs=[whole, block], out_specs=[out] * 4
        ),
        out_shape=[jax.ShapeDtypeStruct((ROWS, COLS), F32)]
        + [jax.ShapeDtypeStruct((ROWS, COLS), BF16)] * 3,
        compiler_params=grant(6),
    )(order, base, l1)


def step_kernel(order, own, got, g, m, average, start):
    avg = (own[...] + got[...].astype(F32)) / REPLICAS
    new_m = momentum_rate * m[...] + avg
    new_g = g[...] - outer_rate * (avg + momentum_rate * new_m)
    average[...] = avg
    start[...] = new_g.astype(BF16)


def outer_step(order, own, got, g, m):
    here = pl.BlockSpec((ROWS, COLS), lambda s, o: (0, 0))
    block = pl.BlockSpec((ROWS, COLS), lambda s, o: (o[16], o[24]))
    return pl.pallas_call(
        step_kernel,
        grid_spec=pltpu.PrefetchScalarGridSpec(
            num_scalar_prefetch=1, grid=(1,), in_specs=[here] * 2 + [block] * 2, out_specs=[here] * 2
        ),
        out_shape=[
            jax.ShapeDtypeStruct((ROWS, COLS), F32),
            jax.ShapeDtypeStruct((ROWS, COLS), BF16),
        ],
        compiler_params=grant(4),
    )(order, own, got, g, m)


def join_kernel(*refs):
    *parts, out = refs
    at = 0
    for ref in parts:
        n = ref.shape[0]
        out[at : at + n] = ref[...]
        at += n


def join(*parts):
    n = sum(p.shape[0] for p in parts)
    return pl.pallas_call(
        join_kernel,
        out_shape=jax.ShapeDtypeStruct((n, *parts[0].shape[1:]), parts[0].dtype),
        compiler_params=grant(4),
    )(*parts)


def update_kernel(order, average, average_other, g, m, new_global, new_momentum):
    mine = order[24] == 0
    for h in range(2):
        cols = slice(h * COLS, (h + 1) * COLS)
        avg = jnp.where(mine == (h == 0), average[0], average_other[0])
        new_m = momentum_rate * m[:, cols] + avg
        new_momentum[:, cols] = new_m
        new_global[:, cols] = g[:, cols] - outer_rate * (avg + momentum_rate * new_m)


def update(order, average, average_other, g, m):
    block = pl.BlockSpec((ROWS, KW), lambda s, o: (o[28 + s], 0))
    part = pl.BlockSpec((1, ROWS, COLS), lambda s, o: (s, 0, 0))
    return pl.pallas_call(
        update_kernel,
        grid_spec=pltpu.PrefetchScalarGridSpec(
            num_scalar_prefetch=1,
            grid=(4,),
            in_specs=[part, part, block, block],
            out_specs=[block] * 2,
        ),
        out_shape=[jax.ShapeDtypeStruct((SHARD, KW), F32)] * 2,
        compiler_params=grant(8),
    )(order, average, average_other, g, m)


def hold_kernel(a, b, a_held, b_held, sem):
    copies = []
    for k, (src, dst) in enumerate(((a, a_held), (b, b_held))):
        for h in range(2):
            rows = pl.ds(h * COLS, COLS)
            copies.append(pltpu.make_async_copy(src.at[rows], dst.at[rows], sem.at[2 * k + h]))
            copies[-1].start()
    for copy in copies:
        copy.wait()


def hold(a, b):
    return pl.pallas_call(
        hold_kernel,
        in_specs=[pl.BlockSpec(memory_space=pltpu.HBM)] * 2,
        out_specs=[pl.BlockSpec(memory_space=pltpu.VMEM)] * 2,
        out_shape=[pltpu.VMEM((TOK, D), BF16)] * 2,
        scratch_shapes=[pltpu.SemaphoreType.DMA((4,))],
        compiler_params=grant(1),
    )(in_hbm(a), in_hbm(b))


def keys_kernel(order, tokens, tokens_other, w0, w1, w2, w3, keys, keys_other, weights):
    for d in range(4):
        for z in range(2):
            for k, ref in enumerate((w0, w1, w2, w3)):
                zl = order[12 + (z + (k == 2)) % 2]
                at = order[4 + d] * (2 * SHARD) + zl * SHARD + order[20 + k] * ROWS
                weights[pl.ds(pl.multiple_of(at, ROWS), ROWS), :] = ref[2 * d + z]
    for src, out in ((tokens_other, keys_other), (tokens, keys)):
        out[...] = jnp.dot(src[...], weights[...], preferred_element_type=F32).astype(BF16)


def keys_of(order, tokens, tokens_other, blocks):
    here = pl.BlockSpec(memory_space=pltpu.VMEM)
    return pl.pallas_call(
        keys_kernel,
        in_specs=[pl.BlockSpec(memory_space=pltpu.SMEM)] + [here] * 6,
        out_specs=[here] * 2,
        scratch_shapes=[pltpu.VMEM((D, COLS), BF16)],
        out_shape=[jax.ShapeDtypeStruct((TOK, COLS), BF16)] * 2,
        compiler_params=grant(24),
        cost_estimate=pl.CostEstimate(flops=20 * TOK * D * KW, bytes_accessed=14 << 20, transcendentals=0),
    )(order, tokens, tokens_other, *blocks)


def per_device(local_weights, global_weights, momentum, tokens, key_grad):
    g, m, local = global_weights, momentum, local_weights[0]
    rep, fsdp = lax.axis_index("rep"), lax.axis_index("fsdp")
    core, x, y, zl = rep % 2, rep // 2 % 4, fsdp // 2, fsdp % 2
    four = jnp.arange(4)
    way = 1 - 2 * core
    piece = x ^ (2 * zl)

    def shards_of(y):
        return (y % 4) * 2 + (zl + jnp.arange(2)) % 2

    order = jnp.concatenate(
        [
            shards_of(y + 2),
            shards_of(y - way),
            (y - four) % 4,
            shards_of(y + way),
            shards_of(y),
            (zl + four) % 2,
            (piece + four) % 4,
            (piece - four) % 4,
            core + 0 * four,
            piece ^ four,
        ]
    ).astype(jnp.int32)

    local_other = shift(local, core=1)
    base = base_of(order, g, local)
    own, p1, p2, p3 = pair_sums(order, base, after(local_other, base))
    r1, r2, r3 = (shift(p, x=k + 1) for k, p in enumerate((p1, p2, p3)))

    far_other, direct = grad_parts(order, (1, 2, 3), (1, 2), after(tokens, p1), key_grad)
    far_other_got = shift(far_other, y=1, both_ways=True)
    direct_got = shift(direct, y=-1, both_ways=True)

    chips = own + after(r1, far_other).astype(F32) + r2.astype(F32) + r3.astype(F32)
    sent = chips.astype(BF16)
    tokens_other = shift(after(tokens, sent), core=1)
    total = chips + flip(sent, zh=1).astype(F32)
    sent = total.astype(BF16)
    on_other, here_other, far_own = grad_parts(
        order, (9, 11, 0), (1, 1, 1), after(tokens, sent), key_grad
    )
    average, start = outer_step(order, total, after(flip(sent, zh=2), far_own), g, m)

    start_other = shift(start, zl=1, x=2)
    on_other = on_other + after(far_other_got, start)
    on_other_got = shift(on_other, y=1, both_ways=True)
    average_1 = flip(after(average, start), x=1)
    pair = join(start[None], after(start_other, average_1)[None])
    pair, tokens_other, direct_got = lax.optimization_barrier((pair, tokens_other, direct_got))
    average_1 = join(average[None], average_1[None])
    average_2 = flip(after(average_1, pair), x=2)
    shards = join(after(pair, average_2), *(shift(pair, y=k) for k in (1, 2, 3)))
    blocks = [shards, shift(shards, x=1), across(shards), shift(shards, x=-1)]

    average_2 = join(average_1, average_2)
    average_other = shift(average_2, core=1)
    new_global, new_momentum = update(order, average_2, average_other, g, m)

    grad_sent = here_other[0].astype(F32) + direct_got[1].astype(F32) + after(on_other_got, shards)[0].astype(F32)
    grad_got = shift(grad_sent.astype(BF16), zl=1)
    far_own_got = shift(after(far_own, shards), y=1, both_ways=True)
    on_own, here_own = grad_parts(order, (8, 10), (1, 1), after(tokens, average_other), key_grad)
    on_own_got = shift(on_own + far_own_got, y=1, both_ways=True)

    tokens, tokens_other = hold(after(tokens, shards), tokens_other)

    grad_kept = here_own[0].astype(F32) + direct_got[0].astype(F32) + on_own_got[0].astype(F32)
    weight_grad = (grad_kept + grad_got.astype(F32)).astype(BF16)[None]

    *blocks, new_global, tokens = lax.optimization_barrier((*blocks, new_global, tokens))
    keys, keys_other = keys_of(order, tokens, tokens_other, blocks)
    keys_got = after(shift(keys_other, core=1), weight_grad)
    inner_keys = jnp.where(
        core == 0,
        jnp.concatenate([keys, keys_got], axis=1),
        jnp.concatenate([keys_got, keys], axis=1),
    )
    return (new_global, new_momentum, inner_keys, weight_grad)


def solution(mesh):
    placed = (
        P("rep", "fsdp", None),
        P("fsdp", None),
        P("fsdp", None),
        P(("rep", "fsdp"), None),
        P(("rep", "fsdp"), None),
    )
    return jax.shard_map(
        per_device,
        mesh=mesh,
        in_specs=placed,
        out_specs=(
            P("fsdp", None),
            P("fsdp", None),
            P(("rep", "fsdp"), None),
            P("rep", "fsdp", None),
        ),
        check_vma=False,
    )
```

```python
import functools
import itertools

import jax
import jax.numpy as jnp
from jax import lax
from jax.experimental import pallas as pl
from jax.experimental.pallas import tpu as pltpu
from jax.sharding import PartitionSpec as P

momentum_rate = 0.9
outer_rate = 0.7

F32, BF16 = jnp.float32, jnp.bfloat16
AXES = ("rep", "fsdp")
SIZES = (4, 4, 2, 4, 2)
REPLICAS = 32
D, KW, SHARD = 5120, 512, 640
TOK = 512
ROWS, COLS = 160, 256


def send(value, target):
    pairs = []
    for place in itertools.product(*map(range, SIZES)):
        index = [0, 0]
        for k, where in enumerate((place, target(*place))):
            for p, size in zip(where, SIZES):
                index[k] = index[k] * size + p % size
        pairs.append(tuple(index))
    return lax.ppermute(value, AXES, pairs)


def shift(value, zh=0, x=0, core=0, y=0, zl=0, both_ways=False):
    def target(a, b, c, d, e):
        sign = -1 if both_ways and c == 1 else 1
        return a + sign * zh, b + sign * x, c + core, d + sign * y, e + zl

    return send(value, target)


def flip(value, zh=0, x=0):
    return send(value, lambda a, b, c, d, e: (a ^ zh, b ^ x, c, d, e))


def across(value):
    return send(value, lambda a, b, c, d, e: (a - 1 if e == 0 else a + 1, b, c, d, 1 - e))


def after(value, *others):
    return lax.optimization_barrier((value, *others))[0]


def grant(mib):
    return pltpu.CompilerParams(vmem_limit_bytes=mib << 20)


def in_hbm(value):
    return pltpu.with_memory_space_constraint(value, pltpu.HBM)


def grad_kernel(at, sizes, order, tokens, key_grad, *refs):
    outs, held, held_grad, sem = refs[: len(sizes)], *refs[len(sizes) :]
    copies = [pltpu.make_async_copy(key_grad, held_grad, sem.at[len(at)])]
    for k, i in enumerate(at):
        columns = pl.ds(pl.multiple_of(order[i] * SHARD, SHARD), SHARD)
        copies.append(pltpu.make_async_copy(tokens.at[:, columns], held.at[k], sem.at[k]))
    for copy in copies:
        copy.start()
    copies[0].wait()
    places = [(out, j) for out, n in zip(outs, sizes) for j in range(n)]
    for k, (out, j) in enumerate(places):
        copies[k + 1].wait()
        out[j] = lax.dot_general(
            held[k], held_grad[...], (((0,), (0,)), ((), ())), preferred_element_type=F32
        ).astype(BF16)


def grad_parts(order, at, sizes, tokens, key_grad):
    n = len(at)
    here = pl.BlockSpec(memory_space=pltpu.VMEM)
    hbm = pl.BlockSpec(memory_space=pltpu.HBM)
    return pl.pallas_call(
        functools.partial(grad_kernel, at, sizes),
        in_specs=[pl.BlockSpec(memory_space=pltpu.SMEM), hbm, hbm],
        out_specs=[here] * len(sizes),
        out_shape=[jax.ShapeDtypeStruct((k, SHARD, KW), BF16) for k in sizes],
        scratch_shapes=[
            pltpu.VMEM((n, TOK, SHARD), BF16),
            pltpu.VMEM((TOK, KW), BF16),
            pltpu.SemaphoreType.DMA((n + 1,)),
        ],
        compiler_params=grant(5 + 3 * n),
        cost_estimate=pl.CostEstimate(
            flops=2 * n * TOK * SHARD * KW, bytes_accessed=n * 1310720, transcendentals=0
        ),
    )(order, in_hbm(tokens), in_hbm(key_grad))


def base_kernel(order, g, l, base):
    base[...] = 2.0 * g[...] - l[...].astype(F32)


def base_of(order, g, l):
    block = pl.BlockSpec((SHARD, COLS), lambda s, o: (0, o[24]))
    return pl.pallas_call(
        base_kernel,
        grid_spec=pltpu.PrefetchScalarGridSpec(
            num_scalar_prefetch=1,
            grid=(1,),
            in_specs=[block] * 2,
            out_specs=pl.BlockSpec((SHARD, COLS), lambda s, o: (0, 0)),
        ),
        out_shape=jax.ShapeDtypeStruct((SHARD, COLS), F32),
        compiler_params=grant(6),
    )(order, in_hbm(g), in_hbm(l))


def pair_kernel(order, base, l1, own, p1, p2, p3):
    for k, ref in enumerate((own, p1, p2, p3)):
        rows = pl.ds(pl.multiple_of(order[16 + k] * ROWS, ROWS), ROWS)
        ref[...] = (base[rows, :] - l1[rows, :].astype(F32)).astype(ref.dtype)


def pair_sums(order, base, l1):
    whole = pl.BlockSpec((SHARD, COLS), lambda s, o: (0, 0))
    block = pl.BlockSpec((SHARD, COLS), lambda s, o: (0, o[24]))
    out = pl.BlockSpec((ROWS, COLS), lambda s, o: (0, 0))
    return pl.pallas_call(
        pair_kernel,
        grid_spec=pltpu.PrefetchScalarGridSpec(
            num_scalar_prefetch=1, grid=(1,), in_specs=[whole, block], out_specs=[out] * 4
        ),
        out_shape=[jax.ShapeDtypeStruct((ROWS, COLS), F32)]
        + [jax.ShapeDtypeStruct((ROWS, COLS), BF16)] * 3,
        compiler_params=grant(6),
    )(order, base, l1)


def step_kernel(order, own, got, g, m, average, start):
    avg = (own[...] + got[...].astype(F32)) / REPLICAS
    new_m = momentum_rate * m[...] + avg
    new_g = g[...] - outer_rate * (avg + momentum_rate * new_m)
    average[...] = avg
    start[...] = new_g.astype(BF16)


def outer_step(order, own, got, g, m):
    here = pl.BlockSpec((ROWS, COLS), lambda s, o: (0, 0))
    block = pl.BlockSpec((ROWS, COLS), lambda s, o: (o[16], o[24]))
    return pl.pallas_call(
        step_kernel,
        grid_spec=pltpu.PrefetchScalarGridSpec(
            num_scalar_prefetch=1, grid=(1,), in_specs=[here] * 2 + [block] * 2, out_specs=[here] * 2
        ),
        out_shape=[
            jax.ShapeDtypeStruct((ROWS, COLS), F32),
            jax.ShapeDtypeStruct((ROWS, COLS), BF16),
        ],
        compiler_params=grant(4),
    )(order, own, got, g, m)


def join_kernel(*refs):
    *parts, out = refs
    at = 0
    for ref in parts:
        n = ref.shape[0]
        out[at : at + n] = ref[...]
        at += n


def join(*parts):
    n = sum(p.shape[0] for p in parts)
    return pl.pallas_call(
        join_kernel,
        out_shape=jax.ShapeDtypeStruct((n, *parts[0].shape[1:]), parts[0].dtype),
        compiler_params=grant(4),
    )(*parts)


def update_kernel(order, average, average_other, g, m, new_global, new_momentum):
    mine = order[24] == 0
    for j in range(2):
        at = order[28 + 2 * pl.program_id(0) + j] % 2 * ROWS
        rows = pl.ds(pl.multiple_of(at, ROWS), ROWS)
        for h in range(2):
            cols = slice(h * COLS, (h + 1) * COLS)
            avg = jnp.where(mine == (h == 0), average[j], average_other[j])
            new_m = momentum_rate * m[rows, cols] + avg
            new_momentum[rows, cols] = new_m
            new_global[rows, cols] = g[rows, cols] - outer_rate * (avg + momentum_rate * new_m)


def update(order, average, average_other, g, m):
    block = pl.BlockSpec((2 * ROWS, KW), lambda s, o: (o[28 + 2 * s] // 2, 0))
    part = pl.BlockSpec((2, ROWS, COLS), lambda s, o: (s, 0, 0))
    return pl.pallas_call(
        update_kernel,
        grid_spec=pltpu.PrefetchScalarGridSpec(
            num_scalar_prefetch=1,
            grid=(2,),
            in_specs=[part, part, block, block],
            out_specs=[block] * 2,
        ),
        out_shape=[jax.ShapeDtypeStruct((SHARD, KW), F32)] * 2,
        compiler_params=grant(10),
    )(order, average, average_other, g, m)


def hold_kernel(a, b, a_held, b_held, sem):
    copies = []
    for k, (src, dst) in enumerate(((a, a_held), (b, b_held))):
        for h in range(2):
            rows = pl.ds(h * COLS, COLS)
            copies.append(pltpu.make_async_copy(src.at[rows], dst.at[rows], sem.at[2 * k + h]))
            copies[-1].start()
    for copy in copies:
        copy.wait()


def hold(a, b):
    return pl.pallas_call(
        hold_kernel,
        in_specs=[pl.BlockSpec(memory_space=pltpu.HBM)] * 2,
        out_specs=[pl.BlockSpec(memory_space=pltpu.VMEM)] * 2,
        out_shape=[pltpu.VMEM((TOK, D), BF16)] * 2,
        scratch_shapes=[pltpu.SemaphoreType.DMA((4,))],
        compiler_params=grant(1),
    )(in_hbm(a), in_hbm(b))


def keys_kernel(order, tokens, tokens_other, w0, w1, w2, w3, keys, keys_other, weights):
    for d in range(4):
        for z in range(2):
            for k, ref in enumerate((w0, w1, w2, w3)):
                zl = order[12 + (z + (k == 2)) % 2]
                at = order[4 + d] * (2 * SHARD) + zl * SHARD + order[20 + k] * ROWS
                weights[pl.ds(pl.multiple_of(at, ROWS), ROWS), :] = ref[2 * d + z]
    for src, out in ((tokens_other, keys_other), (tokens, keys)):
        out[...] = jnp.dot(src[...], weights[...], preferred_element_type=F32).astype(BF16)


def keys_of(order, tokens, tokens_other, blocks):
    here = pl.BlockSpec(memory_space=pltpu.VMEM)
    return pl.pallas_call(
        keys_kernel,
        in_specs=[pl.BlockSpec(memory_space=pltpu.SMEM)] + [here] * 6,
        out_specs=[here] * 2,
        scratch_shapes=[pltpu.VMEM((D, COLS), BF16)],
        out_shape=[jax.ShapeDtypeStruct((TOK, COLS), BF16)] * 2,
        compiler_params=grant(24),
        cost_estimate=pl.CostEstimate(flops=20 * TOK * D * KW, bytes_accessed=14 << 20, transcendentals=0),
    )(order, tokens, tokens_other, *blocks)


def per_device(local_weights, global_weights, momentum, tokens, key_grad):
    g, m, local = global_weights, momentum, local_weights[0]
    rep, fsdp = lax.axis_index("rep"), lax.axis_index("fsdp")
    core, x, y, zl = rep % 2, rep // 2 % 4, fsdp // 2, fsdp % 2
    four = jnp.arange(4)
    way = 1 - 2 * core
    piece = x ^ (2 * zl)

    def shards_of(y):
        return (y % 4) * 2 + (zl + jnp.arange(2)) % 2

    order = jnp.concatenate(
        [
            shards_of(y + 2),
            shards_of(y - way),
            (y - four) % 4,
            shards_of(y + way),
            shards_of(y),
            (zl + four) % 2,
            (piece + four) % 4,
            (piece - four) % 4,
            core + 0 * four,
            piece ^ four,
        ]
    ).astype(jnp.int32)

    local_other = shift(local, core=1)
    base = base_of(order, g, local)
    own, p1, p2, p3 = pair_sums(order, base, after(local_other, base))
    r1, r2, r3 = (shift(p, x=k + 1) for k, p in enumerate((p1, p2, p3)))

    far_other, direct = grad_parts(order, (1, 2, 3), (1, 2), after(tokens, p1), key_grad)
    far_other_got = shift(far_other, y=1, both_ways=True)
    direct_got = shift(direct, y=-1, both_ways=True)

    chips = own + after(r1, far_other).astype(F32) + r2.astype(F32) + r3.astype(F32)
    sent = chips.astype(BF16)
    tokens_other = shift(after(tokens, sent), core=1)
    total = chips + flip(sent, zh=1).astype(F32)
    sent = total.astype(BF16)
    on_other, here_other, far_own = grad_parts(
        order, (9, 11, 0), (1, 1, 1), after(tokens, sent), key_grad
    )
    average, start = outer_step(order, total, after(flip(sent, zh=2), far_own), g, m)

    start_other = shift(start, zl=1, x=2)
    on_other = on_other + after(far_other_got, start)
    on_other_got = shift(on_other, y=1, both_ways=True)
    average_1 = flip(after(average, start), x=1)
    pair = join(start[None], after(start_other, average_1)[None])
    pair, tokens_other, direct_got = lax.optimization_barrier((pair, tokens_other, direct_got))
    average_1 = join(average[None], average_1[None])
    average_2 = flip(after(average_1, pair), x=2)
    shards = join(after(pair, average_2), *(shift(pair, y=k) for k in (1, 2, 3)))
    blocks = [shards, shift(shards, x=1), across(shards), shift(shards, x=-1)]

    average_2 = join(average_1, average_2)
    average_other = shift(average_2, core=1)
    new_global, new_momentum = update(order, average_2, average_other, g, m)

    grad_sent = here_other[0].astype(F32) + direct_got[1].astype(F32) + after(on_other_got, shards)[0].astype(F32)
    grad_got = shift(grad_sent.astype(BF16), zl=1)
    far_own_got = shift(after(far_own, shards), y=1, both_ways=True)
    on_own, here_own = grad_parts(order, (8, 10), (1, 1), after(tokens, average_other), key_grad)
    on_own_got = shift(on_own + far_own_got, y=1, both_ways=True)

    tokens, tokens_other = hold(after(tokens, shards), tokens_other)

    grad_kept = here_own[0].astype(F32) + direct_got[0].astype(F32) + on_own_got[0].astype(F32)
    weight_grad = (grad_kept + grad_got.astype(F32)).astype(BF16)[None]

    *blocks, new_global, tokens = lax.optimization_barrier((*blocks, new_global, tokens))
    keys, keys_other = keys_of(order, tokens, tokens_other, blocks)
    keys_got = after(shift(keys_other, core=1), weight_grad)
    inner_keys = jnp.where(
        core == 0,
        jnp.concatenate([keys, keys_got], axis=1),
        jnp.concatenate([keys_got, keys], axis=1),
    )
    return (new_global, new_momentum, inner_keys, weight_grad)


def solution(mesh):
    placed = (
        P("rep", "fsdp", None),
        P("fsdp", None),
        P("fsdp", None),
        P(("rep", "fsdp"), None),
        P(("rep", "fsdp"), None),
    )
    return jax.shard_map(
        per_device,
        mesh=mesh,
        in_specs=placed,
        out_specs=(
            P("fsdp", None),
            P("fsdp", None),
            P(("rep", "fsdp"), None),
            P("rep", "fsdp", None),
        ),
        check_vma=False,
    )
```

```python
import functools
import itertools

import jax
import jax.numpy as jnp
from jax import lax
from jax.experimental import pallas as pl
from jax.experimental.pallas import tpu as pltpu
from jax.sharding import PartitionSpec as P

momentum_rate = 0.9
outer_rate = 0.7

F32, BF16 = jnp.float32, jnp.bfloat16
AXES = ("rep", "fsdp")
SIZES = (4, 4, 2, 4, 2)
REPLICAS = 32
D, KW, SHARD = 5120, 512, 640
TOK = 512
ROWS, COLS = 160, 256


def send(value, target):
    pairs = []
    for place in itertools.product(*map(range, SIZES)):
        index = [0, 0]
        for k, where in enumerate((place, target(*place))):
            for p, size in zip(where, SIZES):
                index[k] = index[k] * size + p % size
        pairs.append(tuple(index))
    return lax.ppermute(value, AXES, pairs)


def shift(value, zh=0, x=0, core=0, y=0, zl=0, both_ways=False):
    def target(a, b, c, d, e):
        sign = -1 if both_ways and c == 1 else 1
        return a + sign * zh, b + sign * x, c + core, d + sign * y, e + zl

    return send(value, target)


def flip(value, zh=0, x=0):
    return send(value, lambda a, b, c, d, e: (a ^ zh, b ^ x, c, d, e))


def across(value):
    return send(value, lambda a, b, c, d, e: (a - 1 if e == 0 else a + 1, b, c, d, 1 - e))


def after(value, *others):
    return lax.optimization_barrier((value, *others))[0]


def grant(mib):
    return pltpu.CompilerParams(vmem_limit_bytes=mib << 20)


def in_hbm(value):
    return pltpu.with_memory_space_constraint(value, pltpu.HBM)


def grad_kernel(at, sizes, order, tokens, key_grad, *refs):
    outs, held, held_grad, sem = refs[: len(sizes)], *refs[len(sizes) :]
    copies = [pltpu.make_async_copy(key_grad, held_grad, sem.at[len(at)])]
    for k, i in enumerate(at):
        columns = pl.ds(pl.multiple_of(order[i] * SHARD, SHARD), SHARD)
        copies.append(pltpu.make_async_copy(tokens.at[:, columns], held.at[k], sem.at[k]))
    for copy in copies:
        copy.start()
    copies[0].wait()
    places = [(out, j) for out, n in zip(outs, sizes) for j in range(n)]
    for k, (out, j) in enumerate(places):
        copies[k + 1].wait()
        out[j] = lax.dot_general(
            held[k], held_grad[...], (((0,), (0,)), ((), ())), preferred_element_type=F32
        ).astype(BF16)


def grad_parts(order, at, sizes, tokens, key_grad):
    n = len(at)
    here = pl.BlockSpec(memory_space=pltpu.VMEM)
    hbm = pl.BlockSpec(memory_space=pltpu.HBM)
    return pl.pallas_call(
        functools.partial(grad_kernel, at, sizes),
        in_specs=[pl.BlockSpec(memory_space=pltpu.SMEM), hbm, hbm],
        out_specs=[here] * len(sizes),
        out_shape=[jax.ShapeDtypeStruct((k, SHARD, KW), BF16) for k in sizes],
        scratch_shapes=[
            pltpu.VMEM((n, TOK, SHARD), BF16),
            pltpu.VMEM((TOK, KW), BF16),
            pltpu.SemaphoreType.DMA((n + 1,)),
        ],
        compiler_params=grant(5 + 3 * n),
        cost_estimate=pl.CostEstimate(
            flops=2 * n * TOK * SHARD * KW, bytes_accessed=n * 1310720, transcendentals=0
        ),
    )(order, in_hbm(tokens), in_hbm(key_grad))


def base_kernel(order, g, l, base):
    base[...] = 2.0 * g[...] - l[...].astype(F32)


def base_of(order, g, l):
    block = pl.BlockSpec((SHARD, COLS), lambda s, o: (0, o[24]))
    return pl.pallas_call(
        base_kernel,
        grid_spec=pltpu.PrefetchScalarGridSpec(
            num_scalar_prefetch=1,
            grid=(1,),
            in_specs=[block] * 2,
            out_specs=pl.BlockSpec((SHARD, COLS), lambda s, o: (0, 0)),
        ),
        out_shape=jax.ShapeDtypeStruct((SHARD, COLS), F32),
        compiler_params=grant(6),
    )(order, in_hbm(g), in_hbm(l))


def pair_kernel(order, base, l1, own, p1, p2, p3):
    for k, ref in enumerate((own, p1, p2, p3)):
        rows = pl.ds(pl.multiple_of(order[16 + k] * ROWS, ROWS), ROWS)
        ref[...] = (base[rows, :] - l1[rows, :].astype(F32)).astype(ref.dtype)


def pair_sums(order, base, l1):
    whole = pl.BlockSpec((SHARD, COLS), lambda s, o: (0, 0))
    block = pl.BlockSpec((SHARD, COLS), lambda s, o: (0, o[24]))
    out = pl.BlockSpec((ROWS, COLS), lambda s, o: (0, 0))
    return pl.pallas_call(
        pair_kernel,
        grid_spec=pltpu.PrefetchScalarGridSpec(
            num_scalar_prefetch=1, grid=(1,), in_specs=[whole, block], out_specs=[out] * 4
        ),
        out_shape=[jax.ShapeDtypeStruct((ROWS, COLS), F32)]
        + [jax.ShapeDtypeStruct((ROWS, COLS), BF16)] * 3,
        compiler_params=grant(6),
    )(order, base, l1)


def step_kernel(order, own, got, g, m, average, start):
    avg = (own[...] + got[...].astype(F32)) / REPLICAS
    new_m = momentum_rate * m[...] + avg
    new_g = g[...] - outer_rate * (avg + momentum_rate * new_m)
    average[...] = avg
    start[...] = new_g.astype(BF16)


def outer_step(order, own, got, g, m):
    here = pl.BlockSpec((ROWS, COLS), lambda s, o: (0, 0))
    block = pl.BlockSpec((ROWS, COLS), lambda s, o: (o[16], o[24]))
    return pl.pallas_call(
        step_kernel,
        grid_spec=pltpu.PrefetchScalarGridSpec(
            num_scalar_prefetch=1, grid=(1,), in_specs=[here] * 2 + [block] * 2, out_specs=[here] * 2
        ),
        out_shape=[
            jax.ShapeDtypeStruct((ROWS, COLS), F32),
            jax.ShapeDtypeStruct((ROWS, COLS), BF16),
        ],
        compiler_params=grant(4),
    )(order, own, got, g, m)


def join_kernel(*refs):
    *parts, out = refs
    at = 0
    for ref in parts:
        n = ref.shape[0]
        out[at : at + n] = ref[...]
        at += n


def join(*parts):
    n = sum(p.shape[0] for p in parts)
    return pl.pallas_call(
        join_kernel,
        out_shape=jax.ShapeDtypeStruct((n, *parts[0].shape[1:]), parts[0].dtype),
        compiler_params=grant(4),
    )(*parts)


def update_kernel(order, average, average_other, g, m, new_global, new_momentum):
    mine = order[24] == 0
    for j in range(2):
        at = order[28 + 2 * pl.program_id(0) + j] % 2 * ROWS
        rows = pl.ds(pl.multiple_of(at, ROWS), ROWS)
        for h in range(2):
            cols = slice(h * COLS, (h + 1) * COLS)
            avg = jnp.where(mine == (h == 0), average[j], average_other[j])
            new_m = momentum_rate * m[rows, cols] + avg
            new_momentum[rows, cols] = new_m
            new_global[rows, cols] = g[rows, cols] - outer_rate * (avg + momentum_rate * new_m)


def update(order, average, average_other, g, m):
    block = pl.BlockSpec((2 * ROWS, KW), lambda s, o: (o[28 + 2 * s] // 2, 0))
    part = pl.BlockSpec((2, ROWS, COLS), lambda s, o: (s, 0, 0))
    return pl.pallas_call(
        update_kernel,
        grid_spec=pltpu.PrefetchScalarGridSpec(
            num_scalar_prefetch=1,
            grid=(2,),
            in_specs=[part, part, block, block],
            out_specs=[block] * 2,
        ),
        out_shape=[jax.ShapeDtypeStruct((SHARD, KW), F32)] * 2,
        compiler_params=grant(10),
    )(order, average, average_other, g, m)


def hold_kernel(a, b, a_held, b_held, sem):
    copies = []
    for k, (src, dst) in enumerate(((a, a_held), (b, b_held))):
        for h in range(2):
            rows = pl.ds(h * COLS, COLS)
            copies.append(pltpu.make_async_copy(src.at[rows], dst.at[rows], sem.at[2 * k + h]))
            copies[-1].start()
    for copy in copies:
        copy.wait()


def hold(a, b):
    return pl.pallas_call(
        hold_kernel,
        in_specs=[pl.BlockSpec(memory_space=pltpu.HBM)] * 2,
        out_specs=[pl.BlockSpec(memory_space=pltpu.VMEM)] * 2,
        out_shape=[pltpu.VMEM((TOK, D), BF16)] * 2,
        scratch_shapes=[pltpu.SemaphoreType.DMA((4,))],
        compiler_params=grant(1),
    )(in_hbm(a), in_hbm(b))


def keys_kernel(order, tokens, tokens_other, w0, w1, w2, w3, keys, keys_other, weights):
    for d in range(4):
        for z in range(2):
            for k, ref in enumerate((w0, w1, w2, w3)):
                zl = order[12 + (z + (k == 2)) % 2]
                at = order[4 + d] * (2 * SHARD) + zl * SHARD + order[20 + k] * ROWS
                weights[pl.ds(pl.multiple_of(at, ROWS), ROWS), :] = ref[2 * d + z]
    keys_other[...] = jnp.dot(
        tokens_other[...], weights[...], preferred_element_type=F32
    ).astype(BF16)
    mine = pl.ds(pl.multiple_of(order[24] * COLS, COLS), COLS)
    keys[:, mine] = jnp.dot(tokens[...], weights[...], preferred_element_type=F32).astype(BF16)


def keys_of(order, tokens, tokens_other, blocks):
    here = pl.BlockSpec(memory_space=pltpu.VMEM)
    return pl.pallas_call(
        keys_kernel,
        in_specs=[pl.BlockSpec(memory_space=pltpu.SMEM)] + [here] * 6,
        out_specs=[here] * 2,
        scratch_shapes=[pltpu.VMEM((D, COLS), BF16)],
        out_shape=[jax.ShapeDtypeStruct((TOK, n), BF16) for n in (KW, COLS)],
        compiler_params=grant(24),
        cost_estimate=pl.CostEstimate(flops=20 * TOK * D * KW, bytes_accessed=14 << 20, transcendentals=0),
    )(order, tokens, tokens_other, *blocks)


def per_device(local_weights, global_weights, momentum, tokens, key_grad):
    g, m, local = global_weights, momentum, local_weights[0]
    rep, fsdp = lax.axis_index("rep"), lax.axis_index("fsdp")
    core, x, y, zl = rep % 2, rep // 2 % 4, fsdp // 2, fsdp % 2
    four = jnp.arange(4)
    way = 1 - 2 * core
    piece = x ^ (2 * zl)

    def shards_of(y):
        return (y % 4) * 2 + (zl + jnp.arange(2)) % 2

    order = jnp.concatenate(
        [
            shards_of(y + 2),
            shards_of(y - way),
            (y - four) % 4,
            shards_of(y + way),
            shards_of(y),
            (zl + four) % 2,
            (piece + four) % 4,
            (piece - four) % 4,
            core + 0 * four,
            piece ^ four,
        ]
    ).astype(jnp.int32)

    local_other = shift(local, core=1)
    base = base_of(order, g, local)
    own, p1, p2, p3 = pair_sums(order, base, after(local_other, base))
    r1, r2, r3 = (shift(p, x=k + 1) for k, p in enumerate((p1, p2, p3)))

    far_other, direct = grad_parts(order, (1, 2, 3), (1, 2), after(tokens, p1), key_grad)
    far_other_got = shift(far_other, y=1, both_ways=True)
    direct_got = shift(direct, y=-1, both_ways=True)

    chips = own + after(r1, far_other).astype(F32) + r2.astype(F32) + r3.astype(F32)
    sent = chips.astype(BF16)
    tokens_other = shift(after(tokens, sent), core=1)
    total = chips + flip(sent, zh=1).astype(F32)
    sent = total.astype(BF16)
    on_other, here_other, far_own = grad_parts(
        order, (9, 11, 0), (1, 1, 1), after(tokens, sent), key_grad
    )
    average, start = outer_step(order, total, after(flip(sent, zh=2), far_own), g, m)

    start_other = shift(start, zl=1, x=2)
    on_other = on_other + after(far_other_got, start)
    on_other_got = shift(on_other, y=1, both_ways=True)
    average_1 = flip(after(average, start), x=1)
    pair = join(start[None], after(start_other, average_1)[None])
    pair, tokens_other, direct_got = lax.optimization_barrier((pair, tokens_other, direct_got))
    average_1 = join(average[None], average_1[None])
    average_2 = flip(after(average_1, pair), x=2)
    shards = join(after(pair, average_2), *(shift(pair, y=k) for k in (1, 2, 3)))
    blocks = [shards, shift(shards, x=1), across(shards), shift(shards, x=-1)]

    average_2 = join(average_1, average_2)
    average_other = shift(average_2, core=1)
    new_global, new_momentum = update(order, average_2, average_other, g, m)

    grad_sent = here_other[0].astype(F32) + direct_got[1].astype(F32) + after(on_other_got, shards)[0].astype(F32)
    grad_got = shift(grad_sent.astype(BF16), zl=1)
    far_own_got = shift(after(far_own, shards), y=1, both_ways=True)
    on_own, here_own = grad_parts(order, (8, 10), (1, 1), after(tokens, average_other), key_grad)
    on_own_got = shift(on_own + far_own_got, y=1, both_ways=True)

    tokens, tokens_other = hold(after(tokens, shards), tokens_other)

    grad_kept = here_own[0].astype(F32) + direct_got[0].astype(F32) + on_own_got[0].astype(F32)
    weight_grad = (grad_kept + grad_got.astype(F32)).astype(BF16)[None]

    *blocks, new_global, tokens = lax.optimization_barrier((*blocks, new_global, tokens))
    keys, keys_other = keys_of(order, tokens, tokens_other, blocks)
    keys_got = after(shift(keys_other, core=1), weight_grad)
    inner_keys = lax.dynamic_update_slice(keys, keys_got, (0, (1 - core) * COLS))
    return (new_global, new_momentum, inner_keys, weight_grad)


def solution(mesh):
    placed = (
        P("rep", "fsdp", None),
        P("fsdp", None),
        P("fsdp", None),
        P(("rep", "fsdp"), None),
        P(("rep", "fsdp"), None),
    )
    return jax.shard_map(
        per_device,
        mesh=mesh,
        in_specs=placed,
        out_specs=(
            P("fsdp", None),
            P("fsdp", None),
            P(("rep", "fsdp"), None),
            P("rep", "fsdp", None),
        ),
        check_vma=False,
    )
```
